32 devices in a mesh: seq: 8 (over z, y), tp: 4 (over x, core).
Axes of the slice: x: 2, y: 2, z: 4, core: 2. Of those that a mesh axis runs over, the one named last changes fastest.
Arguments:
- hidden_in: bfloat16 [4096, 2560], P('seq', 'tp'), may hold values from -24 to 24, as said below
- query_proj: bfloat16 [2560, 2048], P(None, 'tp'), may hold values from -0.125 to 0.125
- key_projection: bfloat16 [2560, 1024], P(None, 'tp'), may hold values from -0.125 to 0.125
- value_projection: bfloat16 [2560, 1024], P(None, 'tp'), may hold values from -0.125 to 0.125
- output_proj: bfloat16 [2048, 2560], P('tp'), may hold values from -0.125 to 0.125
- out_cotangent: bfloat16 [4096, 2560], P('seq', 'tp'), may hold values from -6 to 6
- doc_start: int32 [4096], P('seq'), may hold values from 0 to 4095, as said below
Outputs:
- hidden_grad: bfloat16 [4096, 2560], P('seq', 'tp')
- query_proj_grad: float32 [2560, 2048], P('seq', 'tp')
- key_proj_grad: float32 [2560, 1024], P('seq', 'tp')
- value_proj_grad: float32 [2560, 1024], P('seq', 'tp')
- output_proj_grad: float32 [2048, 2560], P('tp', 'seq')
The draws below stay inside these ranges and needn't reach their ends.
Inputs may be any that keep to these rules, and one draw needn't show every extreme that they name: hidden_in's entries lie within the range. doc_start[0] = 0; doc_start[t] <= t; doc_start is constant within a document and equals t at each token t that begins one, so it never falls; the last token begins a document of its own.
All inputs are finite; a program needn't handle non-finite values.
Results may differ from the reference program's by a relative error of at most 0.035.
Values may be sent and summed in bfloat16 or wider, within the bound.
A program may use at most 128 MiB of HBM per device.

```python
import math
import jax
import jax.numpy as jnp
from jax import lax

MODEL_WIDTH = 2560
QUERY_HEADS = 8
KEY_VALUE_HEADS = 4
HEAD_SIZE = 256
LOOKBACK_SPAN = 1024
TOKENS_PER_SHARD = 512
SEQUENCE_TOKENS = 4096


def draw_hidden_in(key, part):
    first_key = jax.random.fold_in(key, 0)
    base = jax.random.normal(first_key, (SEQUENCE_TOKENS, MODEL_WIDTH), jnp.float32)
    return jnp.clip(base, -6.0, 6.0).astype(jnp.bfloat16)


def draw_doc_start(key, part):
    first_key, second_key = jax.random.split(key)
    blocks = SEQUENCE_TOKENS // TOKENS_PER_SHARD
    region = jax.random.randint(first_key, (blocks,), 0, 4)
    short_gap = max(4, LOOKBACK_SPAN // 16)
    long_gap = 2 * LOOKBACK_SPAN
    gaps = jnp.repeat(jnp.where(region == 0, short_gap, long_gap).astype(jnp.int32), TOKENS_PER_SHARD)
    draws = jax.random.randint(second_key, (SEQUENCE_TOKENS,), 0, 1 << 20)
    positions = jnp.arange(SEQUENCE_TOKENS, dtype=jnp.int32)
    begins = (draws % gaps == 0) | (positions == 0) | (positions == SEQUENCE_TOKENS - 1)
    return lax.cummax(jnp.where(begins, positions, 0).astype(jnp.int32), axis=0)


def raised(result, rng, source, target, parts, factor):
    def block_of(position):
        return (jnp.arange(result.shape[position]) // (result.shape[position] // parts)).reshape((-1,) + (1,) * (result.ndim - 1 - position))

    first = jax.random.permutation(rng, parts)[block_of(target)]
    far = (block_of(target) + parts // 2) % parts
    return jnp.where((block_of(source) == first) | (block_of(source) == far), factor * result, result)


def levels(stream_key, dims, cuts, least, top_value):
    loudness = 1.0
    for axis_at, parts in cuts:
        steps = jax.random.uniform(jax.random.fold_in(jax.random.fold_in(stream_key, 6), axis_at), (parts,), jnp.float32, least / len(cuts), top_value / len(cuts))
        loudness = loudness * jnp.repeat(jnp.exp(steps), dims[axis_at] // parts).reshape((-1,) + (1,) * (len(dims) - 1 - axis_at))
    return loudness


def scatter_about(own_key, shape, deviation, most, cuts=(), held_as=jnp.bfloat16):
    loudness = levels(own_key, shape, cuts, -0.22, 0.18) if cuts else 1.0
    drawn = jax.random.normal(own_key, shape, jnp.float32) * deviation * loudness
    return jnp.minimum(jnp.maximum(drawn, -most), most).astype(held_as)


def heavy_noise(key, shape, scale, most, shards, heavy, kind=jnp.bfloat16):
    array = scale * jax.random.normal(key, shape, jnp.float32)
    if shards:
        array = array * levels(key, shape, shards, -0.22, 0.18)
    return jnp.clip(raised(array, jax.random.fold_in(key, 3), *heavy), -most, most).astype(kind)


def setup_inputs(seed: int = 0) -> dict:
    key_list = jax.random.split(jax.random.key(seed), 8)
    hidden_in = draw_hidden_in(jax.random.fold_in(key_list[7], 71), 0)
    query_proj = scatter_about(key_list[1], (MODEL_WIDTH, QUERY_HEADS * HEAD_SIZE), MODEL_WIDTH ** -0.5, 0.125, ((1, 4),))
    key_projection = scatter_about(key_list[2], (MODEL_WIDTH, KEY_VALUE_HEADS * HEAD_SIZE), MODEL_WIDTH ** -0.5, 0.125, ((1, 4),))
    value_projection = scatter_about(key_list[3], (MODEL_WIDTH, KEY_VALUE_HEADS * HEAD_SIZE), MODEL_WIDTH ** -0.5, 0.125, ((1, 4),))
    output_proj = scatter_about(key_list[4], (QUERY_HEADS * HEAD_SIZE, MODEL_WIDTH), (QUERY_HEADS * HEAD_SIZE) ** -0.5, 0.125, ((0, 4),))
    out_cotangent = heavy_noise(key_list[5], (SEQUENCE_TOKENS, MODEL_WIDTH), 1.0, 6.0, ((0, 8), (1, 4)), (0, 1, 8, 2.0))
    doc_start = draw_doc_start(jax.random.fold_in(key_list[7], 71), 0)
    return {"hidden_in": hidden_in, "query_proj": query_proj, "key_projection": key_projection, "value_projection": value_projection, "output_proj": output_proj, "out_cotangent": out_cotangent, "doc_start": doc_start}


def rounded(value):
    return lax.optimization_barrier(value.astype(jnp.bfloat16)).astype(jnp.float32)

def reference(hidden_in, query_proj, key_projection, value_projection, output_proj, out_cotangent, doc_start):
    query_group = QUERY_HEADS // KEY_VALUE_HEADS
    blocks = SEQUENCE_TOKENS // TOKENS_PER_SHARD
    window_extent = LOOKBACK_SPAN + TOKENS_PER_SHARD
    query_matrix = jnp.dot(hidden_in, query_proj, preferred_element_type=jnp.float32).astype(jnp.bfloat16)
    keys = jnp.dot(hidden_in, key_projection, preferred_element_type=jnp.float32).astype(jnp.bfloat16)
    values = jnp.dot(hidden_in, value_projection, preferred_element_type=jnp.float32).astype(jnp.bfloat16)
    attention_gradient = jnp.dot(out_cotangent, output_proj.T, preferred_element_type=jnp.float32).astype(jnp.bfloat16)
    pad_amount = jnp.zeros((LOOKBACK_SPAN, KEY_VALUE_HEADS * HEAD_SIZE), jnp.bfloat16)
    padded_keys = jnp.concatenate([pad_amount, keys], 0)
    padded_values = jnp.concatenate([pad_amount, values], 0)
    local = jnp.arange(TOKENS_PER_SHARD, dtype=jnp.int32)
    key_local = jnp.arange(window_extent, dtype=jnp.int32)

    def one_block(carry, block):
        key_acc, value_acc = carry
        start_position = (block * TOKENS_PER_SHARD).astype(jnp.int32)
        rows_of_query = lax.dynamic_slice_in_dim(query_matrix, start_position, TOKENS_PER_SHARD, 0).reshape(TOKENS_PER_SHARD, KEY_VALUE_HEADS, query_group, HEAD_SIZE).astype(jnp.float32)
        key_tile = lax.dynamic_slice_in_dim(padded_keys, start_position, window_extent, 0).reshape(window_extent, KEY_VALUE_HEADS, HEAD_SIZE).astype(jnp.float32)
        value_tile = lax.dynamic_slice_in_dim(padded_values, start_position, window_extent, 0).reshape(window_extent, KEY_VALUE_HEADS, HEAD_SIZE).astype(jnp.float32)
        gradient_rows = lax.dynamic_slice_in_dim(attention_gradient, start_position, TOKENS_PER_SHARD, 0).reshape(TOKENS_PER_SHARD, KEY_VALUE_HEADS, query_group, HEAD_SIZE).astype(jnp.float32)
        starts = lax.dynamic_slice_in_dim(doc_start, start_position, TOKENS_PER_SHARD, 0)
        q_pos = start_position + local
        k_pos = start_position - LOOKBACK_SPAN + key_local
        allowed = (k_pos[None, :] >= starts[:, None]) & (k_pos[None, :] <= q_pos[:, None]) & (q_pos[:, None] - k_pos[None, :] < LOOKBACK_SPAN)
        logits = jnp.einsum('ikgd,jkd->kgij', rows_of_query, key_tile) / math.sqrt(HEAD_SIZE)
        masked = jnp.where(allowed, logits, -jnp.inf)
        row_max = lax.optimization_barrier(jnp.max(masked, -1, keepdims=True))
        row_sum = lax.optimization_barrier(jnp.sum(jnp.exp(masked - row_max), -1, keepdims=True))
        log_norm = row_max + jnp.log(row_sum)
        probs = jnp.where(allowed, jnp.exp(logits - log_norm), 0.0)
        probability_reduced = rounded(probs)
        attended = jnp.einsum('kgij,jkd->ikgd', probability_reduced, value_tile)
        attn_low = rounded(attended)
        delta = jnp.transpose(lax.optimization_barrier(jnp.sum(gradient_rows * attn_low, -1)), (1, 2, 0))
        prob_grad = jnp.einsum('ikgd,jkd->kgij', gradient_rows, value_tile)
        logit_gradient = rounded(probs * (prob_grad - delta[..., None]) / math.sqrt(HEAD_SIZE))
        query_grad = jnp.einsum('kgij,jkd->ikgd', logit_gradient, key_tile).astype(jnp.bfloat16)
        key_portion = jnp.einsum('fqwc,wfqu->cfu', logit_gradient, rows_of_query).reshape(window_extent, KEY_VALUE_HEADS * HEAD_SIZE)
        value_portion = jnp.einsum('fqwc,wfqu->cfu', probability_reduced, gradient_rows).reshape(window_extent, KEY_VALUE_HEADS * HEAD_SIZE)
        key_acc = lax.dynamic_update_slice_in_dim(key_acc, lax.dynamic_slice_in_dim(key_acc, start_position, window_extent, 0) + key_portion, start_position, 0)
        value_acc = lax.dynamic_update_slice_in_dim(value_acc, lax.dynamic_slice_in_dim(value_acc, start_position, window_extent, 0) + value_portion, start_position, 0)
        return ((key_acc, value_acc), (query_grad.reshape(TOKENS_PER_SHARD, QUERY_HEADS * HEAD_SIZE), attn_low.astype(jnp.bfloat16).reshape(TOKENS_PER_SHARD, QUERY_HEADS * HEAD_SIZE)))
    zero_accumulator = jnp.zeros((SEQUENCE_TOKENS + LOOKBACK_SPAN, KEY_VALUE_HEADS * HEAD_SIZE), jnp.float32)
    (key_acc, value_acc), (query_blocks, attn_blocks) = lax.scan(one_block, (zero_accumulator, zero_accumulator), jnp.arange(blocks, dtype=jnp.int32))
    query_grad = query_blocks.reshape(SEQUENCE_TOKENS, QUERY_HEADS * HEAD_SIZE)
    attention = attn_blocks.reshape(SEQUENCE_TOKENS, QUERY_HEADS * HEAD_SIZE)
    key_grad = key_acc[LOOKBACK_SPAN:].astype(jnp.bfloat16)
    value_grad = value_acc[LOOKBACK_SPAN:].astype(jnp.bfloat16)
    hidden_grad = (jnp.dot(query_grad, query_proj.T, preferred_element_type=jnp.float32) + jnp.dot(key_grad, key_projection.T, preferred_element_type=jnp.float32) + jnp.dot(value_grad, value_projection.T, preferred_element_type=jnp.float32)).astype(jnp.bfloat16)
    query_proj_grad = jnp.dot(hidden_in.T, query_grad, preferred_element_type=jnp.float32)
    key_proj_grad = jnp.dot(hidden_in.T, key_grad, preferred_element_type=jnp.float32)
    value_proj_grad = jnp.dot(hidden_in.T, value_grad, preferred_element_type=jnp.float32)
    output_proj_grad = jnp.dot(attention.T, out_cotangent, preferred_element_type=jnp.float32)
    return (hidden_grad, query_proj_grad, key_proj_grad, value_proj_grad, output_proj_grad)
```

```python
import math

import jax
import jax.numpy as jnp
from jax import lax
from jax.sharding import PartitionSpec as P

HEAD_SIZE = 256
LOOKBACK_SPAN = 1024
BF16 = jnp.bfloat16
F32 = jnp.float32


def dot(left, right):
    return jnp.dot(left, right, preferred_element_type=F32)


def transposed_dot(left, right):
    return lax.dot_general(left, right, (((0,), (0,)), ((), ())), preferred_element_type=F32)


def right_transposed_dot(left, right):
    return lax.dot_general(left, right, (((1,), (1,)), ((), ())), preferred_element_type=F32)


def swap(value, axis, bit):
    count = lax.axis_size(axis)
    return lax.ppermute(value, axis, [(i, i ^ bit) for i in range(count)])


def shift(value, steps):
    count = lax.axis_size("seq")
    return lax.ppermute(
        value, "seq", [(i, i + steps) for i in range(count) if 0 <= i + steps < count]
    )


def gather_features(block):
    me = lax.axis_index("tp")
    high, low = me // 2, me % 2
    other = swap(block, "tp", 2)
    first = jnp.where(high == 0, block, other)
    second = jnp.where(high == 0, other, block)
    near_first, near_second = swap(first, "tp", 1), swap(second, "tp", 1)
    return jnp.concatenate(
        [
            jnp.where(low == 0, first, near_first),
            jnp.where(low == 0, near_first, first),
            jnp.where(low == 0, second, near_second),
            jnp.where(low == 0, near_second, second),
        ],
        axis=1,
    )


def chain_sum(parts):
    levels = parts.shape[0]
    level = lax.axis_index("seq") // 2
    up = down = None

    def block(index):
        return lax.dynamic_index_in_dim(parts, jnp.clip(index, 0, levels - 1), 0, keepdims=False)

    def added(value, arrived):
        if arrived is None:
            return value
        return (value.astype(F32) + arrived.astype(F32)).astype(BF16)

    for step in range(levels - 1):
        gap = levels - 1 - step
        up_value = added(block(level + gap), up)
        down_value = added(block(level - gap), down)
        ups, downs = [], []
        for z in range(levels):
            for y in range(2):
                if z <= step:
                    ups.append((2 * z + y, 2 * z + 2 + y))
                if z >= gap:
                    downs.append((2 * z + y, 2 * z - 2 + y))
        up = lax.ppermute(up_value, "seq", ups)
        down = lax.ppermute(down_value, "seq", downs)
    total = block(level).astype(F32)
    if up is not None:
        total = total + up.astype(F32) + down.astype(F32)
    return total


def per_device(
    hidden_in, query_proj, key_projection, value_projection, output_proj, out_cotangent, doc_start
):
    tok_rows, shard_width = hidden_in.shape
    reach = LOOKBACK_SPAN // tok_rows
    seq_count = lax.axis_size("seq")
    tp_count = lax.axis_size("tp")
    levels = seq_count // 2
    my_index = lax.axis_index("seq")
    parity = my_index % 2
    width = shard_width * tp_count
    piece = width // seq_count

    def halves(array):
        split = array.reshape(tok_rows, -1, 2, piece)
        even = split[:, :, 0].reshape(tok_rows, -1)
        odd = split[:, :, 1].reshape(tok_rows, -1)
        mine = jnp.where(parity == 0, even, odd)
        theirs = jnp.where(parity == 0, odd, even)
        return mine, theirs

    full_hidden = gather_features(hidden_in)
    key_values = dot(full_hidden, jnp.concatenate([key_projection, value_projection], 1)).astype(BF16)
    halo = [shift(key_values, offset) for offset in range(1, reach + 1)]
    full_cotangent = gather_features(out_cotangent)
    query_matrix = dot(full_hidden, query_proj).astype(BF16)
    attention_gradient = right_transposed_dot(full_cotangent, output_proj).astype(BF16)

    hidden_theirs = swap(halves(hidden_in)[1], "seq", 1)
    cot_theirs = swap(halves(out_cotangent)[1], "seq", 1)
    hidden_pair = jnp.concatenate(
        [halves(full_hidden)[0], gather_features(hidden_theirs)], 0
    )
    cot_pair = jnp.concatenate([halves(full_cotangent)[0], gather_features(cot_theirs)], 0)

    kv_width = key_projection.shape[1]
    kv_heads = kv_width // HEAD_SIZE
    group = query_proj.shape[1] // kv_width
    span = (reach + 1) * tok_rows
    window = jnp.concatenate(halo[::-1] + [key_values], 0)
    scale = math.sqrt(HEAD_SIZE)
    q_pos = my_index * tok_rows + jnp.arange(tok_rows, dtype=jnp.int32)
    k_pos = (my_index - reach) * tok_rows + jnp.arange(span, dtype=jnp.int32)
    allowed = (
        (k_pos[None, :] >= doc_start[:, None])
        & (k_pos[None, :] <= q_pos[:, None])
        & (q_pos[:, None] - k_pos[None, :] < LOOKBACK_SPAN)
    )
    attention, query_grad, key_parts, value_parts = [], [], [], []
    for kv in range(kv_heads):
        keys = window[:, kv * HEAD_SIZE : (kv + 1) * HEAD_SIZE]
        values = window[:, kv_width + kv * HEAD_SIZE : kv_width + (kv + 1) * HEAD_SIZE]
        key_total = value_total = 0.0
        for member in range(group):
            at = (kv * group + member) * HEAD_SIZE
            queries = query_matrix[:, at : at + HEAD_SIZE]
            grads = attention_gradient[:, at : at + HEAD_SIZE]
            logits = jnp.where(allowed, right_transposed_dot(queries, keys) / scale, -jnp.inf)
            weights = jnp.exp(logits - jnp.max(logits, -1, keepdims=True))
            probs = weights * (1.0 / jnp.sum(weights, -1, keepdims=True))
            probs_low = probs.astype(BF16)
            attended = dot(probs_low, values).astype(BF16)
            delta = jnp.sum(grads.astype(F32) * attended.astype(F32), -1, keepdims=True)
            prob_grad = right_transposed_dot(grads, values)
            logit_grad = (probs * (prob_grad - delta) / scale).astype(BF16)
            attention.append(attended)
            query_grad.append(dot(logit_grad, keys).astype(BF16))
            key_total = key_total + transposed_dot(logit_grad, queries)
            value_total = value_total + transposed_dot(probs_low, grads)
        key_parts.append(key_total)
        value_parts.append(value_total)
    attention = jnp.concatenate(attention, 1)
    query_grad = jnp.concatenate(query_grad, 1)
    parts = jnp.concatenate(key_parts + value_parts, 1)
    kv_total = parts[reach * tok_rows :]
    for offset in range(1, reach + 1):
        start = (reach - offset) * tok_rows
        kv_total = kv_total + shift(
            parts[start : start + tok_rows].astype(BF16), -offset
        ).astype(F32)
    kv_grad = kv_total.astype(BF16)

    attention_pair = jnp.concatenate([attention, swap(attention, "seq", 1)], 0)
    query_pair = jnp.concatenate([query_grad, swap(query_grad, "seq", 1)], 0)
    kv_pair = jnp.concatenate([kv_grad, swap(kv_grad, "seq", 1)], 0)

    def summed(left, right):
        return chain_sum(
            transposed_dot(left, right).astype(BF16).reshape(levels, piece, right.shape[1])
        )

    output_proj_grad = summed(cot_pair, attention_pair).T
    query_proj_grad = summed(hidden_pair, query_pair)
    kv_proj_grad = summed(hidden_pair, kv_pair)

    term = (
        right_transposed_dot(query_grad, query_proj)
        + right_transposed_dot(kv_grad[:, :kv_width], key_projection)
        + right_transposed_dot(kv_grad[:, kv_width:], value_projection)
    ).astype(BF16)
    me = lax.axis_index("tp")
    blocks = [term[:, i * shard_width : (i + 1) * shard_width] for i in range(tp_count)]
    high, low = me // 2, me % 2
    near = [
        jnp.where(low == 0, blocks[2 * i], blocks[2 * i + 1]).astype(F32)
        + swap(jnp.where(low == 0, blocks[2 * i + 1], blocks[2 * i]), "tp", 1).astype(F32)
        for i in range(2)
    ]
    far = swap(jnp.where(high == 0, near[1], near[0]).astype(BF16), "tp", 2)
    hidden_grad = (jnp.where(high == 0, near[0], near[1]) + far.astype(F32)).astype(BF16)
    return (
        hidden_grad,
        query_proj_grad,
        kv_proj_grad[:, :kv_width],
        kv_proj_grad[:, kv_width:],
        output_proj_grad,
    )


def solution(mesh):
    placed = (
        P("seq", "tp"),
        P(None, "tp"),
        P(None, "tp"),
        P(None, "tp"),
        P("tp", None),
        P("seq", "tp"),
        P("seq"),
    )
    return jax.shard_map(
        per_device,
        mesh=mesh,
        in_specs=placed,
        out_specs=(P("seq", "tp"), P("seq", "tp"), P("seq", "tp"), P("seq", "tp"), P("tp", "seq")),
        check_vma=False,
    )
```

```python
import functools
import math

import jax
import jax.numpy as jnp
from jax import lax
from jax.experimental import pallas as pl
from jax.experimental.pallas import tpu as pltpu
from jax.sharding import PartitionSpec as P

HEAD_SIZE = 256
LOOKBACK_SPAN = 1024
BF16 = jnp.bfloat16
F32 = jnp.float32


def dot(left, right):
    return jnp.dot(left, right, preferred_element_type=F32)


def transposed_dot(left, right):
    return lax.dot_general(left, right, (((0,), (0,)), ((), ())), preferred_element_type=F32)


def right_transposed_dot(left, right):
    return lax.dot_general(left, right, (((1,), (1,)), ((), ())), preferred_element_type=F32)


def swap(value, axis, bit):
    count = lax.axis_size(axis)
    return lax.ppermute(value, axis, [(i, i ^ bit) for i in range(count)])


def shift(value, steps):
    count = lax.axis_size("seq")
    return lax.ppermute(
        value, "seq", [(i, i + steps) for i in range(count) if 0 <= i + steps < count]
    )


def gather_features(block):
    me = lax.axis_index("tp")
    high, low = me // 2, me % 2
    other = swap(block, "tp", 2)
    first = jnp.where(high == 0, block, other)
    second = jnp.where(high == 0, other, block)
    near_first, near_second = swap(first, "tp", 1), swap(second, "tp", 1)
    return jnp.concatenate(
        [
            jnp.where(low == 0, first, near_first),
            jnp.where(low == 0, near_first, first),
            jnp.where(low == 0, second, near_second),
            jnp.where(low == 0, near_second, second),
        ],
        axis=1,
    )


def remote(source, target, send, recv, axis, index):
    return pltpu.make_async_remote_copy(
        src_ref=source,
        dst_ref=target,
        send_sem=send,
        recv_sem=recv,
        device_id={axis: index},
        device_id_type=pl.DeviceIdType.MESH,
    )


def greet(barrier, peers):
    for axis, index, here in peers:

        @pl.when(here)
        def _():
            pl.semaphore_signal(
                barrier, inc=1, device_id={axis: index}, device_id_type=pl.DeviceIdType.MESH
            )

    pl.semaphore_wait(barrier, sum(jnp.where(here, 1, 0) for _, _, here in peers))


def exchange_kernel(
    count, reach, pair, kv_own, halo, pair_near, kv_grad, kv_near,
    landed, total, swap_send, swap_recv, halo_send, halo_recv,
):
    me = lax.axis_index("seq")
    near = me + 1 - 2 * lax.rem(me, 2)
    peers = []
    for offset in range(1, reach + 1):
        peers.append(("seq", me - offset, me >= offset))
        peers.append(("seq", me + offset, me + offset < count))
    greet(pltpu.get_barrier_semaphore(), peers)

    def back(offset):
        return remote(
            halo.at[offset - 1], landed.at[offset - 1],
            halo_send.at[offset - 1], halo_recv.at[offset - 1], "seq", me - offset,
        )

    for offset in range(reach, 0, -1):

        @pl.when(me >= offset)
        def _():
            back(offset).start()

    pair_copy = remote(pair, pair_near, swap_send.at[0], swap_recv.at[0], "seq", near)
    pair_copy.start()
    total[...] = kv_own[...]
    for offset in range(reach, 0, -1):

        @pl.when(me + offset < count)
        def _():
            back(offset).wait_recv()
            total[...] += landed[offset - 1].astype(F32)

    kv_grad[...] = total[...].astype(BF16)
    kv_copy = remote(kv_grad, kv_near, swap_send.at[1], swap_recv.at[1], "seq", near)
    kv_copy.start()
    pair_copy.wait()
    kv_copy.wait()
    for offset in range(1, reach + 1):

        @pl.when(me >= offset)
        def _():
            back(offset).wait_send()


def exchange(pair, kv_own, halo):
    count = lax.axis_size("seq")
    reach = halo.shape[0]
    vmem = pl.BlockSpec(memory_space=pltpu.VMEM)
    return pl.pallas_call(
        functools.partial(exchange_kernel, count, reach),
        out_shape=[
            jax.ShapeDtypeStruct(pair.shape, BF16),
            jax.ShapeDtypeStruct(kv_own.shape, BF16),
            jax.ShapeDtypeStruct(kv_own.shape, BF16),
        ],
        in_specs=[vmem] * 3,
        out_specs=[vmem] * 3,
        scratch_shapes=[
            pltpu.VMEM(halo.shape, BF16),
            pltpu.VMEM(kv_own.shape, F32),
            pltpu.SemaphoreType.DMA((2,)),
            pltpu.SemaphoreType.DMA((2,)),
            pltpu.SemaphoreType.DMA((reach,)),
            pltpu.SemaphoreType.DMA((reach,)),
        ],
        compiler_params=pltpu.CompilerParams(
            collective_id=1, has_side_effects=True, vmem_limit_bytes=40 * 2**20
        ),
    )(pair, kv_own, halo)


def sum_kernel(
    levels, parts_a, parts_b, parts_c, term, out_a, out_b, out_c, hidden,
    up_tx, up_rx, down_tx, down_rx, near_rx, far_tx, far_rx,
    up_send, up_recv, down_send, down_recv, hid_send, hid_recv,
):
    parts = (parts_a, parts_b, parts_c)
    outs = (out_a, out_b, out_c)
    me = lax.axis_index("seq")
    z = me // 2
    tp = lax.axis_index("tp")
    high, low = tp // 2, lax.rem(tp, 2)
    near, far = tp + 1 - 2 * low, tp + 2 - 4 * high
    width = hidden.shape[1]
    always = tp >= 0
    greet(
        pltpu.get_barrier_semaphore(),
        [
            ("seq", me - 2, z >= 1),
            ("seq", me + 2, z <= levels - 2),
            ("tp", near, always),
            ("tp", far, always),
        ],
    )

    def columns(index):
        return pl.ds(pl.multiple_of(index * width, width), width)

    def near_copy(slot):
        half = 1 - high if slot == 0 else high
        return remote(
            term.at[:, columns(2 * half + 1 - low)], near_rx.at[slot],
            hid_send.at[slot], hid_recv.at[slot], "tp", near,
        )

    far_copy = remote(far_tx, far_rx, hid_send.at[2], hid_recv.at[2], "tp", far)

    def up(step, c):
        return remote(
            up_tx.at[step, c], up_rx.at[step, c],
            up_send.at[step, c], up_recv.at[step, c], "seq", me + 2,
        )

    def down(step, c):
        return remote(
            down_tx.at[step, c], down_rx.at[step, c],
            down_send.at[step, c], down_recv.at[step, c], "seq", me - 2,
        )

    near_copy(0).start()
    near_copy(1).start()
    for step in range(levels - 1):
        gap = levels - 1 - step
        for c in range(3):

            @pl.when(z <= step)
            def _():
                @pl.when(z == 0)
                def _():
                    up_tx[step, c] = parts[c][z + gap]

                if step > 0:

                    @pl.when(z >= 1)
                    def _():
                        up(step - 1, c).wait_recv()
                        up_tx[step, c] = (
                            parts[c][z + gap].astype(F32) + up_rx[step - 1, c].astype(F32)
                        ).astype(BF16)

                up(step, c).start()

            @pl.when(z >= gap)
            def _():
                @pl.when(z == levels - 1)
                def _():
                    down_tx[step, c] = parts[c][z - gap]

                if step > 0:

                    @pl.when(z <= levels - 2)
                    def _():
                        down(step - 1, c).wait_recv()
                        down_tx[step, c] = (
                            parts[c][z - gap].astype(F32) + down_rx[step - 1, c].astype(F32)
                        ).astype(BF16)

                down(step, c).start()

        if step == 0:
            near_copy(0).wait_recv()
            far_tx[...] = (
                term[:, columns(2 * (1 - high) + low)].astype(F32) + near_rx[0].astype(F32)
            ).astype(BF16)
            far_copy.start()
    near_copy(1).wait_recv()
    far_copy.wait_recv()
    hidden[...] = (
        term[:, columns(2 * high + low)].astype(F32)
        + near_rx[1].astype(F32)
        + far_rx[...].astype(F32)
    ).astype(BF16)
    last = levels - 2
    for c in range(3):
        outs[c][...] = parts[c][z].astype(F32)

        @pl.when(z >= 1)
        def _():
            up(last, c).wait_recv()
            outs[c][...] += up_rx[last, c].astype(F32)

        @pl.when(z <= levels - 2)
        def _():
            down(last, c).wait_recv()
            outs[c][...] += down_rx[last, c].astype(F32)

    near_copy(0).wait_send()
    near_copy(1).wait_send()
    far_copy.wait_send()
    for step in range(levels - 1):
        for c in range(3):

            @pl.when(z <= step)
            def _():
                up(step, c).wait_send()

            @pl.when(z >= levels - 1 - step)
            def _():
                down(step, c).wait_send()


def final_sums(parts_a, parts_b, parts_c, term):
    levels, rows, columns = parts_a.shape
    shard = term.shape[1] // lax.axis_size("tp")
    vmem = pl.BlockSpec(memory_space=pltpu.VMEM)
    steps = levels - 1
    slots = pltpu.VMEM((steps, 3, rows, columns), BF16)
    block = (term.shape[0], shard)
    sems = pltpu.SemaphoreType.DMA((steps, 3))
    return pl.pallas_call(
        functools.partial(sum_kernel, levels),
        out_shape=[jax.ShapeDtypeStruct((rows, columns), F32)] * 3
        + [jax.ShapeDtypeStruct(block, BF16)],
        in_specs=[vmem] * 4,
        out_specs=[vmem] * 4,
        scratch_shapes=[
            slots, slots, slots, slots,
            pltpu.VMEM((2,) + block, BF16),
            pltpu.VMEM(block, BF16),
            pltpu.VMEM(block, BF16),
            sems, sems, sems, sems,
            pltpu.SemaphoreType.DMA((3,)),
            pltpu.SemaphoreType.DMA((3,)),
        ],
        compiler_params=pltpu.CompilerParams(
            collective_id=2, has_side_effects=True, vmem_limit_bytes=50 * 2**20
        ),
    )(parts_a, parts_b, parts_c, term)


def per_device(
    hidden_in, query_proj, key_projection, value_projection, output_proj, out_cotangent, doc_start
):
    tok_rows, shard_width = hidden_in.shape
    reach = LOOKBACK_SPAN // tok_rows
    seq_count = lax.axis_size("seq")
    tp_count = lax.axis_size("tp")
    levels = seq_count // 2
    my_index = lax.axis_index("seq")
    parity = my_index % 2
    width = shard_width * tp_count
    piece = width // seq_count

    def theirs(array):
        split = array.reshape(tok_rows, -1, 2, piece)
        even = split[:, :, 0].reshape(tok_rows, -1)
        odd = split[:, :, 1].reshape(tok_rows, -1)
        return jnp.where(parity == 0, odd, even)

    full_hidden = gather_features(hidden_in)
    key_values = dot(full_hidden, jnp.concatenate([key_projection, value_projection], 1)).astype(BF16)
    halo = [shift(key_values, offset) for offset in range(1, reach + 1)]
    full_cotangent = gather_features(out_cotangent)
    query_matrix = dot(full_hidden, query_proj).astype(BF16)
    attention_gradient = right_transposed_dot(full_cotangent, output_proj).astype(BF16)

    hidden_near = swap(theirs(hidden_in), "seq", 1)
    cot_near = swap(theirs(out_cotangent), "seq", 1)
    hidden_near, cot_near, query_matrix, attention_gradient = lax.optimization_barrier(
        (hidden_near, cot_near, query_matrix, attention_gradient)
    )
    hidden_near = gather_features(hidden_near)
    cot_near = gather_features(cot_near)

    kv_width = key_projection.shape[1]
    kv_heads = kv_width // HEAD_SIZE
    group = query_proj.shape[1] // kv_width
    span = (reach + 1) * tok_rows
    window = jnp.concatenate(halo[::-1] + [key_values], 0)
    scale = math.sqrt(HEAD_SIZE)
    q_pos = my_index * tok_rows + jnp.arange(tok_rows, dtype=jnp.int32)
    k_pos = (my_index - reach) * tok_rows + jnp.arange(span, dtype=jnp.int32)
    allowed = (
        (k_pos[None, :] >= doc_start[:, None])
        & (k_pos[None, :] <= q_pos[:, None])
        & (q_pos[:, None] - k_pos[None, :] < LOOKBACK_SPAN)
    )
    attention, query_grad, key_parts, value_parts = [], [], [], []
    for kv in range(kv_heads):
        keys = window[:, kv * HEAD_SIZE : (kv + 1) * HEAD_SIZE]
        values = window[:, kv_width + kv * HEAD_SIZE : kv_width + (kv + 1) * HEAD_SIZE]
        key_total = value_total = 0.0
        for member in range(group):
            at = (kv * group + member) * HEAD_SIZE
            queries = query_matrix[:, at : at + HEAD_SIZE]
            grads = attention_gradient[:, at : at + HEAD_SIZE]
            logits = jnp.where(allowed, right_transposed_dot(queries, keys) / scale, -jnp.inf)
            weights = jnp.exp(logits - jnp.max(logits, -1, keepdims=True))
            probs = weights * (1.0 / jnp.sum(weights, -1, keepdims=True))
            probs_low = probs.astype(BF16)
            attended = dot(probs_low, values).astype(BF16)
            delta = jnp.sum(grads.astype(F32) * attended.astype(F32), -1, keepdims=True)
            prob_grad = right_transposed_dot(grads, values)
            logit_grad = (probs * (prob_grad - delta) / scale).astype(BF16)
            attention.append(attended)
            query_grad.append(dot(logit_grad, keys).astype(BF16))
            key_total = key_total + transposed_dot(logit_grad, queries)
            value_total = value_total + transposed_dot(probs_low, grads)
        key_parts.append(key_total)
        value_parts.append(value_total)
    attention = jnp.concatenate(attention, 1)
    query_grad = jnp.concatenate(query_grad, 1)
    parts = jnp.concatenate(key_parts + value_parts, 1)
    halo_back = jnp.stack(
        [
            parts[(reach - offset) * tok_rows : (reach - offset + 1) * tok_rows].astype(BF16)
            for offset in range(1, reach + 1)
        ]
    )
    pair = jnp.concatenate([attention, query_grad], 1)
    pair_near, kv_grad, kv_near = exchange(pair, parts[reach * tok_rows :], halo_back)

    def summed(full, right, near, right_near):
        own = transposed_dot(full, right).reshape(levels, 2, piece, right.shape[1])
        own = jnp.where(parity == 0, own[:, 0], own[:, 1])
        return (own + transposed_dot(near, right_near).reshape(own.shape)).astype(BF16)

    q_width = query_grad.shape[1]
    output_parts = summed(full_cotangent, attention, cot_near, pair_near[:, :q_width])
    query_parts = summed(full_hidden, query_grad, hidden_near, pair_near[:, q_width:])
    kv_parts = summed(full_hidden, kv_grad, hidden_near, kv_near)

    term = (
        right_transposed_dot(query_grad, query_proj)
        + right_transposed_dot(kv_grad[:, :kv_width], key_projection)
        + right_transposed_dot(kv_grad[:, kv_width:], value_projection)
    ).astype(BF16)
    output_grad, query_proj_grad, kv_proj_grad, hidden_grad = final_sums(
        output_parts, query_parts, kv_parts, term
    )
    return (
        hidden_grad,
        query_proj_grad,
        kv_proj_grad[:, :kv_width],
        kv_proj_grad[:, kv_width:],
        output_grad.T,
    )


def solution(mesh):
    placed = (
        P("seq", "tp"),
        P(None, "tp"),
        P(None, "tp"),
        P(None, "tp"),
        P("tp", None),
        P("seq", "tp"),
        P("seq"),
    )
    return jax.shard_map(
        per_device,
        mesh=mesh,
        in_specs=placed,
        out_specs=(P("seq", "tp"), P("seq", "tp"), P("seq", "tp"), P("seq", "tp"), P("tp", "seq")),
        check_vma=False,
    )
```

```python
import functools
import math

import jax
import jax.numpy as jnp
from jax import lax
from jax.experimental import pallas as pl
from jax.experimental.pallas import tpu as pltpu
from jax.sharding import PartitionSpec as P

HEAD_SIZE = 256
LOOKBACK_SPAN = 1024
BF16 = jnp.bfloat16
F32 = jnp.float32


def dot(left, right):
    return jnp.dot(left, right, preferred_element_type=F32)


def transposed_dot(left, right):
    return lax.dot_general(left, right, (((0,), (0,)), ((), ())), preferred_element_type=F32)


def right_transposed_dot(left, right):
    return lax.dot_general(left, right, (((1,), (1,)), ((), ())), preferred_element_type=F32)


def swap(value, axis, bit):
    count = lax.axis_size(axis)
    return lax.ppermute(value, axis, [(i, i ^ bit) for i in range(count)])


def shift(value, steps):
    count = lax.axis_size("seq")
    return lax.ppermute(
        value, "seq", [(i, i + steps) for i in range(count) if 0 <= i + steps < count]
    )


def gather_features(block):
    me = lax.axis_index("tp")
    high, low = me // 2, me % 2
    other = swap(block, "tp", 2)
    first = jnp.where(high == 0, block, other)
    second = jnp.where(high == 0, other, block)
    near_first, near_second = swap(first, "tp", 1), swap(second, "tp", 1)
    return jnp.concatenate(
        [
            jnp.where(low == 0, first, near_first),
            jnp.where(low == 0, near_first, first),
            jnp.where(low == 0, second, near_second),
            jnp.where(low == 0, near_second, second),
        ],
        axis=1,
    )


def remote(source, target, send, recv, axis, index):
    return pltpu.make_async_remote_copy(
        src_ref=source,
        dst_ref=target,
        send_sem=send,
        recv_sem=recv,
        device_id={axis: index},
        device_id_type=pl.DeviceIdType.MESH,
    )


def greet(barrier, peers):
    for axis, index, here in peers:

        @pl.when(here)
        def _():
            pl.semaphore_signal(
                barrier, inc=1, device_id={axis: index}, device_id_type=pl.DeviceIdType.MESH
            )

    pl.semaphore_wait(barrier, sum(jnp.where(here, 1, 0) for _, _, here in peers))


def tail_kernel(
    levels, count, reach,
    attention, query_grad, kv_own, halo, own_t, near_t, cot_near_t, out_base, query_base,
    term_base, kv_weights,
    out_a, out_b, out_c, hidden,
    near_data, landed, total, kv_grad, term, parts, up_tx, up_rx, down_tx, down_rx,
    near_rx, far_tx, far_rx,
    swap_send, swap_recv, halo_send, halo_recv,
    up_send, up_recv, down_send, down_recv, hid_send, hid_recv,
):
    outs = (out_a, out_b, out_c)
    me = lax.axis_index("seq")
    z = me // 2
    beside = me + 1 - 2 * lax.rem(me, 2)
    tp = lax.axis_index("tp")
    high, low = tp // 2, lax.rem(tp, 2)
    near, far = tp + 1 - 2 * low, tp + 2 - 4 * high
    width = hidden.shape[1]
    always = tp >= 0
    peers = [("tp", near, always), ("tp", far, always)]
    for offset in range(1, max(reach, 2) + 1):
        peers.append(("seq", me - offset, me >= offset))
        peers.append(("seq", me + offset, me + offset < count))
    greet(pltpu.get_barrier_semaphore(), peers)

    def columns(index):
        return pl.ds(pl.multiple_of(index * width, width), width)

    def back(offset):
        return remote(
            halo.at[offset - 1], landed.at[offset - 1],
            halo_send.at[offset - 1], halo_recv.at[offset - 1], "seq", me - offset,
        )

    def swapped(slot, source):
        return remote(
            source, near_data.at[slot], swap_send.at[slot], swap_recv.at[slot], "seq", beside
        )

    def near_copy(slot):
        half = 1 - high if slot == 0 else high
        return remote(
            term.at[:, columns(2 * half + 1 - low)], near_rx.at[slot],
            hid_send.at[slot], hid_recv.at[slot], "tp", near,
        )

    far_copy = remote(far_tx, far_rx, hid_send.at[2], hid_recv.at[2], "tp", far)

    def up(step, c):
        return remote(
            up_tx.at[step, c], up_rx.at[step, c],
            up_send.at[step, c], up_recv.at[step, c], "seq", me + 2,
        )

    def down(step, c):
        return remote(
            down_tx.at[step, c], down_rx.at[step, c],
            down_send.at[step, c], down_recv.at[step, c], "seq", me - 2,
        )

    def begin(c):
        @pl.when(z == 0)
        def _():
            for step in range(levels - 1):
                up_tx[step, c] = parts[c, levels - 1 - step]
                up(step, c).start()

        @pl.when(z == levels - 1)
        def _():
            for step in range(levels - 1):
                down_tx[step, c] = parts[c, step]
                down(step, c).start()

    def advance(c, step):
        gap = levels - 1 - step

        @pl.when((z >= 1) & (z <= step))
        def _():
            up(step - 1, c).wait_recv()
            up_tx[step, c] = (
                parts[c, z + gap].astype(F32) + up_rx[step - 1, c].astype(F32)
            ).astype(BF16)
            up(step, c).start()

        @pl.when((z >= gap) & (z <= levels - 2))
        def _():
            down(step - 1, c).wait_recv()
            down_tx[step, c] = (
                parts[c, z - gap].astype(F32) + down_rx[step - 1, c].astype(F32)
            ).astype(BF16)
            down(step, c).start()

    def maybe_advance(c, step):
        if step <= levels - 2:
            advance(c, step)

    def product(c, base, left, slot):
        def body(b, carry):
            parts[c, b] = (base[b] + dot(left[b], near_data[slot])).astype(BF16)
            return carry

        lax.fori_loop(0, levels, body, 0)

    attention_copy = swapped(0, attention)
    query_copy = swapped(1, query_grad)
    kv_copy = swapped(2, kv_grad)
    attention_copy.start()
    for offset in range(reach, 0, -1):

        @pl.when(me >= offset)
        def _():
            back(offset).start()

    attention_copy.wait_recv()
    query_copy.start()
    product(0, out_base, cot_near_t, 0)
    begin(0)
    query_copy.wait_recv()
    product(1, query_base, near_t, 1)
    begin(1)
    maybe_advance(0, 1)

    total[...] = kv_own[...]
    for offset in range(reach, 0, -1):

        @pl.when(me + offset < count)
        def _():
            back(offset).wait_recv()
            total[...] += landed[offset - 1].astype(F32)

    kv_grad[...] = total[...].astype(BF16)
    kv_copy.start()
    maybe_advance(1, 1)

    def term_body(i, carry):
        rows = pl.ds(pl.multiple_of(i * width, width), width)
        term[:, columns(i)] = (
            term_base[:, columns(i)] + right_transposed_dot(kv_grad[...], kv_weights[rows, :])
        ).astype(BF16)
        return carry

    lax.fori_loop(0, term.shape[1] // width, term_body, 0)
    near_copy(0).start()
    near_copy(1).start()

    maybe_advance(0, 2)
    kv_copy.wait_recv()

    def kv_body(b, carry):
        parts[2, b] = (
            dot(own_t[b], kv_grad[...]) + dot(near_t[b], near_data[2])
        ).astype(BF16)
        return carry

    lax.fori_loop(0, levels, kv_body, 0)
    begin(2)
    maybe_advance(1, 2)
    near_copy(0).wait_recv()
    far_tx[...] = (
        term[:, columns(2 * (1 - high) + low)].astype(F32) + near_rx[0].astype(F32)
    ).astype(BF16)
    far_copy.start()
    for step in range(3, levels - 1):
        advance(0, step)
        advance(1, step)
    for step in range(1, levels - 1):
        advance(2, step)
    near_copy(1).wait_recv()
    far_copy.wait_recv()
    hidden[...] = (
        term[:, columns(2 * high + low)].astype(F32)
        + near_rx[1].astype(F32)
        + far_rx[...].astype(F32)
    ).astype(BF16)
    last = levels - 2
    for c in range(3):
        outs[c][...] = parts[c, z].astype(F32)

        @pl.when(z >= 1)
        def _():
            up(last, c).wait_recv()
            outs[c][...] += up_rx[last, c].astype(F32)

        @pl.when(z <= levels - 2)
        def _():
            down(last, c).wait_recv()
            outs[c][...] += down_rx[last, c].astype(F32)

    attention_copy.wait_send()
    query_copy.wait_send()
    kv_copy.wait_send()
    for offset in range(1, reach + 1):

        @pl.when(me >= offset)
        def _():
            back(offset).wait_send()

    near_copy(0).wait_send()
    near_copy(1).wait_send()
    far_copy.wait_send()
    for step in range(levels - 1):
        for c in range(3):

            @pl.when(z <= step)
            def _():
                up(step, c).wait_send()

            @pl.when(z >= levels - 1 - step)
            def _():
                down(step, c).wait_send()


def tail(attention, query_grad, kv_own, halo, own_t, near_t, cot_near_t, out_base, query_base,
         term_base, kv_weights):
    levels, rows, tokens = own_t.shape
    columns = attention.shape[1]
    count = lax.axis_size("seq")
    reach = halo.shape[0]
    shard = term_base.shape[1] // lax.axis_size("tp")
    vmem = pl.BlockSpec(memory_space=pltpu.VMEM)
    steps = levels - 1
    slots = pltpu.VMEM((steps, 3, rows, columns), BF16)
    block = (tokens, shard)
    sems = pltpu.SemaphoreType.DMA((steps, 3))
    three = pltpu.SemaphoreType.DMA((3,))
    some = pltpu.SemaphoreType.DMA((reach,))
    return pl.pallas_call(
        functools.partial(tail_kernel, levels, count, reach),
        out_shape=[jax.ShapeDtypeStruct((rows, columns), F32)] * 3
        + [jax.ShapeDtypeStruct(block, BF16)],
        in_specs=[vmem] * 11,
        out_specs=[vmem] * 4,
        scratch_shapes=[
            pltpu.VMEM((3,) + attention.shape, BF16),
            pltpu.VMEM(halo.shape, BF16),
            pltpu.VMEM(kv_own.shape, F32),
            pltpu.VMEM(kv_own.shape, BF16),
            pltpu.VMEM(term_base.shape, BF16),
            pltpu.VMEM((3, levels, rows, columns), BF16),
            slots, slots, slots, slots,
            pltpu.VMEM((2,) + block, BF16),
            pltpu.VMEM(block, BF16),
            pltpu.VMEM(block, BF16),
            three, three, some, some, sems, sems, sems, sems, three, three,
        ],
        compiler_params=pltpu.CompilerParams(
            collective_id=1, has_side_effects=True, vmem_limit_bytes=56 * 2**20
        ),
    )(attention, query_grad, kv_own, halo, own_t, near_t, cot_near_t, out_base, query_base,
      term_base, kv_weights)


def per_device(
    hidden_in, query_proj, key_projection, value_projection, output_proj, out_cotangent, doc_start
):
    tok_rows, shard_width = hidden_in.shape
    reach = LOOKBACK_SPAN // tok_rows
    seq_count = lax.axis_size("seq")
    tp_count = lax.axis_size("tp")
    levels = seq_count // 2
    my_index = lax.axis_index("seq")
    parity = my_index % 2
    width = shard_width * tp_count
    piece = width // seq_count

    def theirs(array):
        split = array.reshape(tok_rows, -1, 2, piece)
        even = split[:, :, 0].reshape(tok_rows, -1)
        odd = split[:, :, 1].reshape(tok_rows, -1)
        return jnp.where(parity == 0, odd, even)

    full_hidden = gather_features(hidden_in)
    kv_weights = jnp.concatenate([key_projection, value_projection], 1)
    key_values = dot(full_hidden, kv_weights).astype(BF16)
    halo = [shift(key_values, offset) for offset in range(1, reach + 1)]
    full_cotangent = gather_features(out_cotangent)
    query_matrix = dot(full_hidden, query_proj).astype(BF16)
    attention_gradient = right_transposed_dot(full_cotangent, output_proj).astype(BF16)

    hidden_near = swap(theirs(hidden_in), "seq", 1)
    cot_near = swap(theirs(out_cotangent), "seq", 1)
    hidden_near, cot_near, query_matrix, attention_gradient = lax.optimization_barrier(
        (hidden_near, cot_near, query_matrix, attention_gradient)
    )
    hidden_near = gather_features(hidden_near)
    cot_near = gather_features(cot_near)

    kv_width = key_projection.shape[1]
    kv_heads = kv_width // HEAD_SIZE
    group = query_proj.shape[1] // kv_width
    span = (reach + 1) * tok_rows
    window = jnp.concatenate(halo[::-1] + [key_values], 0)
    scale = math.sqrt(HEAD_SIZE)
    q_pos = my_index * tok_rows + jnp.arange(tok_rows, dtype=jnp.int32)
    k_pos = (my_index - reach) * tok_rows + jnp.arange(span, dtype=jnp.int32)
    allowed = (
        (k_pos[None, :] >= doc_start[:, None])
        & (k_pos[None, :] <= q_pos[:, None])
        & (q_pos[:, None] - k_pos[None, :] < LOOKBACK_SPAN)
    )
    attention, query_grad, key_parts, value_parts = [], [], [], []
    for kv in range(kv_heads):
        keys = window[:, kv * HEAD_SIZE : (kv + 1) * HEAD_SIZE]
        values = window[:, kv_width + kv * HEAD_SIZE : kv_width + (kv + 1) * HEAD_SIZE]
        key_total = value_total = 0.0
        for member in range(group):
            at = (kv * group + member) * HEAD_SIZE
            queries = query_matrix[:, at : at + HEAD_SIZE]
            grads = attention_gradient[:, at : at + HEAD_SIZE]
            logits = jnp.where(allowed, right_transposed_dot(queries, keys) / scale, -jnp.inf)
            weights = jnp.exp(logits - jnp.max(logits, -1, keepdims=True))
            probs = weights * (1.0 / jnp.sum(weights, -1, keepdims=True))
            probs_low = probs.astype(BF16)
            attended = dot(probs_low, values).astype(BF16)
            delta = jnp.sum(grads.astype(F32) * attended.astype(F32), -1, keepdims=True)
            prob_grad = right_transposed_dot(grads, values)
            logit_grad = (probs * (prob_grad - delta) / scale).astype(BF16)
            attention.append(attended)
            query_grad.append(dot(logit_grad, keys).astype(BF16))
            key_total = key_total + transposed_dot(logit_grad, queries)
            value_total = value_total + transposed_dot(probs_low, grads)
        key_parts.append(key_total)
        value_parts.append(value_total)
    attention = jnp.concatenate(attention, 1)
    query_grad = jnp.concatenate(query_grad, 1)
    parts = jnp.concatenate(key_parts + value_parts, 1)
    halo_back = jnp.stack(
        [
            parts[(reach - offset) * tok_rows : (reach - offset + 1) * tok_rows].astype(BF16)
            for offset in range(1, reach + 1)
        ]
    )

    def own_rows(array):
        split = array.reshape(levels, 2, piece, array.shape[1])
        return jnp.where(parity == 0, split[:, 0], split[:, 1])

    def near_rows(array):
        return array.T.reshape(levels, piece, tok_rows)

    output_grad, query_proj_grad, kv_proj_grad, hidden_grad = tail(
        attention,
        query_grad,
        parts[reach * tok_rows :],
        halo_back,
        own_rows(full_hidden.T),
        near_rows(hidden_near),
        near_rows(cot_near),
        own_rows(transposed_dot(full_cotangent, attention)),
        own_rows(transposed_dot(full_hidden, query_grad)),
        right_transposed_dot(query_grad, query_proj),
        kv_weights,
    )
    return (
        hidden_grad,
        query_proj_grad,
        kv_proj_grad[:, :kv_width],
        kv_proj_grad[:, kv_width:],
        output_grad.T,
    )


def solution(mesh):
    placed = (
        P("seq", "tp"),
        P(None, "tp"),
        P(None, "tp"),
        P(None, "tp"),
        P("tp", None),
        P("seq", "tp"),
        P("seq"),
    )
    return jax.shard_map(
        per_device,
        mesh=mesh,
        in_specs=placed,
        out_specs=(P("seq", "tp"), P("seq", "tp"), P("seq", "tp"), P("seq", "tp"), P("tp", "seq")),
        check_vma=False,
    )
```

```python
import functools
import math

import jax
import jax.numpy as jnp
from jax import lax
from jax.experimental import pallas as pl
from jax.experimental.pallas import tpu as pltpu
from jax.sharding import PartitionSpec as P

HEAD_SIZE = 256
LOOKBACK_SPAN = 1024
BF16 = jnp.bfloat16
F32 = jnp.float32


def dot(left, right):
    return jnp.dot(left, right, preferred_element_type=F32)


def transposed_dot(left, right):
    return lax.dot_general(left, right, (((0,), (0,)), ((), ())), preferred_element_type=F32)


def right_transposed_dot(left, right):
    return lax.dot_general(left, right, (((1,), (1,)), ((), ())), preferred_element_type=F32)


def swap(value, axis, bit):
    count = lax.axis_size(axis)
    return lax.ppermute(value, axis, [(i, i ^ bit) for i in range(count)])


def shift(value, steps):
    count = lax.axis_size("seq")
    return lax.ppermute(
        value, "seq", [(i, i + steps) for i in range(count) if 0 <= i + steps < count]
    )


def gather_features(block):
    me = lax.axis_index("tp")
    high, low = me // 2, me % 2
    other = swap(block, "tp", 2)
    first = jnp.where(high == 0, block, other)
    second = jnp.where(high == 0, other, block)
    near_first, near_second = swap(first, "tp", 1), swap(second, "tp", 1)
    return jnp.concatenate(
        [
            jnp.where(low == 0, first, near_first),
            jnp.where(low == 0, near_first, first),
            jnp.where(low == 0, second, near_second),
            jnp.where(low == 0, near_second, second),
        ],
        axis=1,
    )


def remote(source, target, send, recv, axis, index):
    return pltpu.make_async_remote_copy(
        src_ref=source,
        dst_ref=target,
        send_sem=send,
        recv_sem=recv,
        device_id={axis: index},
        device_id_type=pl.DeviceIdType.MESH,
    )


def greet(barrier, peers):
    for axis, index, here in peers:

        @pl.when(here)
        def _():
            pl.semaphore_signal(
                barrier, inc=1, device_id={axis: index}, device_id_type=pl.DeviceIdType.MESH
            )

    pl.semaphore_wait(barrier, sum(jnp.where(here, 1, 0) for _, _, here in peers))


def gather_kernel(hidden, cotangent, full_hidden, full_cotangent, send, recv):
    tp = lax.axis_index("tp")
    high, low = tp // 2, lax.rem(tp, 2)
    near, far = tp + 1 - 2 * low, tp + 2 - 4 * high
    width = hidden.shape[1]
    always = tp >= 0
    greet(pltpu.get_barrier_semaphore(), [("tp", near, always), ("tp", far, always)])
    pairs = ((hidden, full_hidden), (cotangent, full_cotangent))

    def columns(index):
        return pl.ds(pl.multiple_of(index * width, width), width)

    def copy(i, kind):
        block, full = pairs[i]
        mine = full.at[:, columns(tp)]
        if kind == 2:
            mine = full.at[:, columns(far)]
            return remote(mine, mine, send.at[kind, i], recv.at[kind, i], "tp", near)
        return remote(
            block, mine, send.at[kind, i], recv.at[kind, i], "tp", far if kind == 0 else near
        )

    for kind in range(2):
        for i in range(2):
            copy(i, kind).start()
    for block, full in pairs:
        full[:, columns(tp)] = block[...]
    for i in range(2):
        copy(i, 0).wait_recv()
        copy(i, 2).start()
    for i in range(2):
        copy(i, 1).wait_recv()
        copy(i, 2).wait_recv()
        for kind in range(3):
            copy(i, kind).wait_send()


def gather_both(hidden, cotangent):
    rows, width = hidden.shape
    full = jax.ShapeDtypeStruct((rows, width * lax.axis_size("tp")), BF16)
    vmem = pl.BlockSpec(memory_space=pltpu.VMEM)
    return pl.pallas_call(
        gather_kernel,
        out_shape=[full, full],
        in_specs=[vmem] * 2,
        out_specs=[vmem] * 2,
        scratch_shapes=[pltpu.SemaphoreType.DMA((3, 2)), pltpu.SemaphoreType.DMA((3, 2))],
        compiler_params=pltpu.CompilerParams(
            collective_id=2, has_side_effects=True, vmem_limit_bytes=16 * 2**20
        ),
    )(hidden, cotangent)


def tail_kernel(
    levels, count, reach,
    attention, query_grad, kv_own, halo, own_t, near_t, cot_near_t, out_base, query_base,
    term_base, kv_weights,
    out_a, out_b, out_c, hidden,
    near_data, landed, total, kv_grad, term, parts, up_tx, up_rx, down_tx, down_rx,
    near_rx, far_tx, far_rx,
    swap_send, swap_recv, halo_send, halo_recv,
    up_send, up_recv, down_send, down_recv, hid_send, hid_recv,
):
    outs = (out_a, out_b, out_c)
    me = lax.axis_index("seq")
    z = me // 2
    beside = me + 1 - 2 * lax.rem(me, 2)
    tp = lax.axis_index("tp")
    high, low = tp // 2, lax.rem(tp, 2)
    near, far = tp + 1 - 2 * low, tp + 2 - 4 * high
    width = hidden.shape[1]
    always = tp >= 0
    peers = [("tp", near, always), ("tp", far, always)]
    for offset in range(1, max(reach, 2) + 1):
        peers.append(("seq", me - offset, me >= offset))
        peers.append(("seq", me + offset, me + offset < count))
    greet(pltpu.get_barrier_semaphore(), peers)

    def columns(index):
        return pl.ds(pl.multiple_of(index * width, width), width)

    def back(offset):
        return remote(
            halo.at[offset - 1], landed.at[offset - 1],
            halo_send.at[offset - 1], halo_recv.at[offset - 1], "seq", me - offset,
        )

    def swapped(slot, source):
        return remote(
            source, near_data.at[slot], swap_send.at[slot], swap_recv.at[slot], "seq", beside
        )

    def near_copy(slot):
        half = 1 - high if slot == 0 else high
        return remote(
            term.at[:, columns(2 * half + 1 - low)], near_rx.at[slot],
            hid_send.at[slot], hid_recv.at[slot], "tp", near,
        )

    far_copy = remote(far_tx, far_rx, hid_send.at[2], hid_recv.at[2], "tp", far)

    def up(step, c):
        return remote(
            up_tx.at[step, c], up_rx.at[step, c],
            up_send.at[step, c], up_recv.at[step, c], "seq", me + 2,
        )

    def down(step, c):
        return remote(
            down_tx.at[step, c], down_rx.at[step, c],
            down_send.at[step, c], down_recv.at[step, c], "seq", me - 2,
        )

    def begin(c):
        @pl.when(z == 0)
        def _():
            for step in range(levels - 1):
                up_tx[step, c] = parts[c, levels - 1 - step]
                up(step, c).start()

        @pl.when(z == levels - 1)
        def _():
            for step in range(levels - 1):
                down_tx[step, c] = parts[c, step]
                down(step, c).start()

    def advance(c, step):
        gap = levels - 1 - step

        @pl.when((z >= 1) & (z <= step))
        def _():
            up(step - 1, c).wait_recv()
            up_tx[step, c] = (
                parts[c, z + gap].astype(F32) + up_rx[step - 1, c].astype(F32)
            ).astype(BF16)
            up(step, c).start()

        @pl.when((z >= gap) & (z <= levels - 2))
        def _():
            down(step - 1, c).wait_recv()
            down_tx[step, c] = (
                parts[c, z - gap].astype(F32) + down_rx[step - 1, c].astype(F32)
            ).astype(BF16)
            down(step, c).start()

    def maybe_advance(c, step):
        if step <= levels - 2:
            advance(c, step)

    def product(c, base, left, slot):
        def body(b, carry):
            parts[c, b] = (base[b].astype(F32) + dot(left[b], near_data[slot])).astype(BF16)
            return carry

        lax.fori_loop(0, levels, body, 0)

    attention_copy = swapped(0, attention)
    query_copy = swapped(1, query_grad)
    kv_copy = swapped(2, kv_grad)
    attention_copy.start()
    for offset in range(reach, 0, -1):

        @pl.when(me >= offset)
        def _():
            back(offset).start()

    attention_copy.wait_recv()
    query_copy.start()
    product(0, out_base, cot_near_t, 0)
    begin(0)
    query_copy.wait_recv()
    product(1, query_base, near_t, 1)
    begin(1)
    maybe_advance(0, 1)

    total[...] = kv_own[...]
    for offset in range(reach, 0, -1):

        @pl.when(me + offset < count)
        def _():
            back(offset).wait_recv()
            total[...] += landed[offset - 1].astype(F32)

    kv_grad[...] = total[...].astype(BF16)
    kv_copy.start()
    maybe_advance(1, 1)

    def term_body(i, carry):
        rows = pl.ds(pl.multiple_of(i * width, width), width)
        term[:, columns(i)] = (
            term_base[:, columns(i)].astype(F32)
            + right_transposed_dot(kv_grad[...], kv_weights[rows, :])
        ).astype(BF16)
        return carry

    lax.fori_loop(0, term.shape[1] // width, term_body, 0)
    near_copy(0).start()
    near_copy(1).start()

    maybe_advance(0, 2)
    kv_copy.wait_recv()

    def kv_body(b, carry):
        parts[2, b] = (
            dot(own_t[b], kv_grad[...]) + dot(near_t[b], near_data[2])
        ).astype(BF16)
        return carry

    lax.fori_loop(0, levels, kv_body, 0)
    begin(2)
    maybe_advance(1, 2)
    near_copy(0).wait_recv()
    far_tx[...] = (
        term[:, columns(2 * (1 - high) + low)].astype(F32) + near_rx[0].astype(F32)
    ).astype(BF16)
    far_copy.start()
    for step in range(3, levels - 1):
        advance(0, step)
        advance(1, step)
    for step in range(1, levels - 1):
        advance(2, step)
    near_copy(1).wait_recv()
    far_copy.wait_recv()
    hidden[...] = (
        term[:, columns(2 * high + low)].astype(F32)
        + near_rx[1].astype(F32)
        + far_rx[...].astype(F32)
    ).astype(BF16)
    last = levels - 2
    for c in range(3):
        outs[c][...] = parts[c, z].astype(F32)

        @pl.when(z >= 1)
        def _():
            up(last, c).wait_recv()
            outs[c][...] += up_rx[last, c].astype(F32)

        @pl.when(z <= levels - 2)
        def _():
            down(last, c).wait_recv()
            outs[c][...] += down_rx[last, c].astype(F32)

    attention_copy.wait_send()
    query_copy.wait_send()
    kv_copy.wait_send()
    for offset in range(1, reach + 1):

        @pl.when(me >= offset)
        def _():
            back(offset).wait_send()

    near_copy(0).wait_send()
    near_copy(1).wait_send()
    far_copy.wait_send()
    for step in range(levels - 1):
        for c in range(3):

            @pl.when(z <= step)
            def _():
                up(step, c).wait_send()

            @pl.when(z >= levels - 1 - step)
            def _():
                down(step, c).wait_send()


def tail(attention, query_grad, kv_own, halo, own_t, near_t, cot_near_t, out_base, query_base,
         term_base, kv_weights):
    levels, rows, tokens = own_t.shape
    columns = attention.shape[1]
    count = lax.axis_size("seq")
    reach = halo.shape[0]
    shard = term_base.shape[1] // lax.axis_size("tp")
    vmem = pl.BlockSpec(memory_space=pltpu.VMEM)
    steps = levels - 1
    slots = pltpu.VMEM((steps, 3, rows, columns), BF16)
    block = (tokens, shard)
    sems = pltpu.SemaphoreType.DMA((steps, 3))
    three = pltpu.SemaphoreType.DMA((3,))
    some = pltpu.SemaphoreType.DMA((reach,))
    return pl.pallas_call(
        functools.partial(tail_kernel, levels, count, reach),
        out_shape=[jax.ShapeDtypeStruct((rows, columns), F32)] * 3
        + [jax.ShapeDtypeStruct(block, BF16)],
        in_specs=[vmem] * 11,
        out_specs=[vmem] * 4,
        scratch_shapes=[
            pltpu.VMEM((3,) + attention.shape, BF16),
            pltpu.VMEM(halo.shape, BF16),
            pltpu.VMEM(kv_own.shape, F32),
            pltpu.VMEM(kv_own.shape, BF16),
            pltpu.VMEM(term_base.shape, BF16),
            pltpu.VMEM((3, levels, rows, columns), BF16),
            slots, slots, slots, slots,
            pltpu.VMEM((2,) + block, BF16),
            pltpu.VMEM(block, BF16),
            pltpu.VMEM(block, BF16),
            three, three, some, some, sems, sems, sems, sems, three, three,
        ],
        compiler_params=pltpu.CompilerParams(
            collective_id=1, has_side_effects=True, vmem_limit_bytes=48 * 2**20
        ),
    )(attention, query_grad, kv_own, halo, own_t, near_t, cot_near_t, out_base, query_base,
      term_base, kv_weights)


def per_device(
    hidden_in, query_proj, key_projection, value_projection, output_proj, out_cotangent, doc_start
):
    tok_rows, shard_width = hidden_in.shape
    reach = LOOKBACK_SPAN // tok_rows
    seq_count = lax.axis_size("seq")
    tp_count = lax.axis_size("tp")
    levels = seq_count // 2
    my_index = lax.axis_index("seq")
    parity = my_index % 2
    width = shard_width * tp_count
    piece = width // seq_count

    def theirs(array):
        split = array.reshape(tok_rows, -1, 2, piece)
        even = split[:, :, 0].reshape(tok_rows, -1)
        odd = split[:, :, 1].reshape(tok_rows, -1)
        return jnp.where(parity == 0, odd, even)

    full_hidden, full_cotangent = gather_both(hidden_in, out_cotangent)
    kv_weights = jnp.concatenate([key_projection, value_projection], 1)
    key_values = dot(full_hidden, kv_weights).astype(BF16)
    halo = [shift(key_values, offset) for offset in range(1, reach + 1)]
    query_matrix = dot(full_hidden, query_proj).astype(BF16)
    attention_gradient = right_transposed_dot(full_cotangent, output_proj).astype(BF16)

    hidden_near = swap(theirs(hidden_in), "seq", 1)
    cot_near = swap(theirs(out_cotangent), "seq", 1)
    hidden_near, cot_near, query_matrix, attention_gradient = lax.optimization_barrier(
        (hidden_near, cot_near, query_matrix, attention_gradient)
    )
    hidden_near = gather_features(hidden_near)
    cot_near = gather_features(cot_near)

    kv_width = key_projection.shape[1]
    kv_heads = kv_width // HEAD_SIZE
    group = query_proj.shape[1] // kv_width
    span = (reach + 1) * tok_rows
    window = jnp.concatenate(halo[::-1] + [key_values], 0)
    scale = math.sqrt(HEAD_SIZE)
    q_pos = my_index * tok_rows + jnp.arange(tok_rows, dtype=jnp.int32)
    k_pos = (my_index - reach) * tok_rows + jnp.arange(span, dtype=jnp.int32)
    allowed = (
        (k_pos[None, :] >= doc_start[:, None])
        & (k_pos[None, :] <= q_pos[:, None])
        & (q_pos[:, None] - k_pos[None, :] < LOOKBACK_SPAN)
    )
    attention, query_grad, key_parts, value_parts = [], [], [], []
    for kv in range(kv_heads):
        keys = window[:, kv * HEAD_SIZE : (kv + 1) * HEAD_SIZE]
        values = window[:, kv_width + kv * HEAD_SIZE : kv_width + (kv + 1) * HEAD_SIZE]
        key_total = value_total = 0.0
        for member in range(group):
            at = (kv * group + member) * HEAD_SIZE
            queries = query_matrix[:, at : at + HEAD_SIZE]
            grads = attention_gradient[:, at : at + HEAD_SIZE]
            logits = jnp.where(allowed, right_transposed_dot(queries, keys) / scale, -jnp.inf)
            weights = jnp.exp(logits - jnp.max(logits, -1, keepdims=True))
            probs = weights * (1.0 / jnp.sum(weights, -1, keepdims=True))
            probs_low = probs.astype(BF16)
            attended = dot(probs_low, values).astype(BF16)
            delta = jnp.sum(grads.astype(F32) * attended.astype(F32), -1, keepdims=True)
            prob_grad = right_transposed_dot(grads, values)
            logit_grad = (probs * (prob_grad - delta) / scale).astype(BF16)
            attention.append(attended)
            query_grad.append(dot(logit_grad, keys).astype(BF16))
            key_total = key_total + transposed_dot(logit_grad, queries)
            value_total = value_total + transposed_dot(probs_low, grads)
        key_parts.append(key_total)
        value_parts.append(value_total)
    attention = jnp.concatenate(attention, 1)
    query_grad = jnp.concatenate(query_grad, 1)
    parts = jnp.concatenate(key_parts + value_parts, 1)
    halo_back = jnp.stack(
        [
            parts[(reach - offset) * tok_rows : (reach - offset + 1) * tok_rows].astype(BF16)
            for offset in range(1, reach + 1)
        ]
    )

    def own_rows(array):
        split = array.reshape(levels, 2, piece, array.shape[1])
        return jnp.where(parity == 0, split[:, 0], split[:, 1])

    def near_rows(array):
        return array.T.reshape(levels, piece, tok_rows)

    output_grad, query_proj_grad, kv_proj_grad, hidden_grad = tail(
        attention,
        query_grad,
        parts[reach * tok_rows :],
        halo_back,
        own_rows(full_hidden.T),
        near_rows(hidden_near),
        near_rows(cot_near),
        own_rows(transposed_dot(full_cotangent, attention).astype(BF16)),
        own_rows(transposed_dot(full_hidden, query_grad).astype(BF16)),
        right_transposed_dot(query_grad, query_proj).astype(BF16),
        kv_weights,
    )
    return (
        hidden_grad,
        query_proj_grad,
        kv_proj_grad[:, :kv_width],
        kv_proj_grad[:, kv_width:],
        output_grad.T,
    )


def solution(mesh):
    placed = (
        P("seq", "tp"),
        P(None, "tp"),
        P(None, "tp"),
        P(None, "tp"),
        P("tp", None),
        P("seq", "tp"),
        P("seq"),
    )
    return jax.shard_map(
        per_device,
        mesh=mesh,
        in_specs=placed,
        out_specs=(P("seq", "tp"), P("seq", "tp"), P("seq", "tp"), P("seq", "tp"), P("tp", "seq")),
        check_vma=False,
    )
```
